32 devices in a mesh: vis: 4 (over y, core), band: 8 (over z, x).
Axes of the slice: x: 2, y: 2, z: 4, core: 2. Of those that a mesh axis runs over, the one named last changes fastest.
Arguments:
- vis_values: float32 [2, 131072], P(None, ('vis', 'band')), may hold values from -6 to 6
- time_block: int32 [131072], P(('vis', 'band')), may hold values from 0 to 7
- block_gains: float32 [2, 8], replicated, may hold values from -4 to 4
- target_tile: int32 [131072, 1], P(('vis', 'band')), may hold values from 0 to 31; in each aligned block of 4096 rows (0 to 4095, 4096 to 8191, ...) at most 256 rows name the same one
- cell_row: int32 [131072], P(('vis', 'band')), may hold values from 0 to 1023
- cell_column: int32 [131072], P(('vis', 'band')), may hold values from 0 to 2047
- offsets: int32 [2, 131072], P(None, ('vis', 'band')), may hold values from 0 to 127
- kernel: float32 [128, 8], replicated, may hold values from 0.1 to 1
Outputs:
- sky_image: float32 [2, 8192, 8192], P(None, ('vis', 'band'))
The draws below stay inside these ranges and needn't reach their ends.
Inputs may be any that keep to these rules, and one draw needn't show every extreme that they name: `target_tile`: among the visibilities of one device (aligned blocks of 4096 rows), no tile is named more than 256 times.
All inputs are finite; a program needn't handle non-finite values.
Results may differ from the reference program's by a relative error of at most 0.0038.
Values sent between devices are 32-bit elements; how exact they have to be, the bound alone decides.
A program may use at most 192 MiB of HBM per device.

```python
import math
import jax
import jax.numpy as jnp
import numpy as np
from jax import lax

GRID = 8192
KSUP = 8
OVER = 128
TBLK = 8
VIS_DEV = 4096
VIS = 131072
TILES = 32
ROWS_BAND = 1024
COLS_BLOCK = 2048
CAP = 256
N_BAND = 8


def plant(values, stream_key, least, largest):
    place = [jax.random.randint(jax.random.fold_in(stream_key, axis), (), 0, length) for axis, length in enumerate(values.shape)]
    widest = values.shape.index(max(values.shape))
    beside = place[:widest] + [(place[widest] + 1) % values.shape[widest]] + place[widest + 1:]
    return values.at[tuple(place)].set(least).at[tuple(beside)].set(largest)


def levels(own_key, dims, split, low, top_value):
    gain, own = 1.0, jax.random.fold_in(own_key, 6)
    for axis_at, shards_of in split:
        steps = jnp.exp(jax.random.uniform(jax.random.fold_in(own, axis_at), (shards_of,), jnp.float32, low / len(split), top_value / len(split)))
        gain = gain * jnp.repeat(steps, dims[axis_at] // shards_of).reshape([-1 if axis == axis_at else 1 for axis in range(len(dims))])
    return gain


def assign_block(stream_key, own, number, rows, count, top, most, skew):
    order = jax.random.permutation(stream_key, count)
    heavy_load, ordinary = portions_of(count, rows * top, most, skew, True), portions_of(count, rows * top, most, skew, False)
    places = jnp.arange(count)

    def named(lengths, rotation):
        used = int((lengths > 0).sum())
        fixed = max(1, used // 4)
        passed = fixed + (places - fixed + rotation * (used - fixed)) % max(1, count - fixed)
        return jnp.zeros((count,), jnp.int32).at[order[jnp.where(places < fixed, places, passed)]].set(jnp.asarray(lengths, jnp.int32))

    lengths = jnp.where(number % 4 == 0, named(heavy_load, number // 4), named(ordinary, number - number // 4 - 1))
    mixed = jax.random.permutation(jax.random.fold_in(own, 3), count)
    donor, receiver = mixed[0:count // 2 * 2:2], mixed[1:count // 2 * 2:2]
    slack = jnp.minimum(lengths[donor] - 1, most - lengths[receiver]) // 2
    slack = jnp.where((donor == order[0]) | (receiver == order[0]) | (lengths[receiver] == 0), 0, jnp.maximum(slack, 0))
    passed = jax.random.randint(jax.random.fold_in(own, 4), (count // 2,), 0, 1 << 20) % (slack + 1)
    lengths = lengths.at[donor].add(-passed).at[receiver].add(passed)
    items = jnp.searchsorted(jnp.cumsum(lengths), jnp.arange(rows * top), side="right").astype(jnp.int32)
    table = items.reshape(top, rows).T
    table = table[jax.random.permutation(jax.random.fold_in(own, 1), rows)]
    rotation = jax.random.randint(jax.random.fold_in(own, 2), (rows, 1), 0, top)
    return jnp.take_along_axis(table, (jnp.arange(top)[None, :] + rotation) % top, axis=1)


def portions_of(count, total, most, slope, full):
    weights = [(1 << 20) // math.isqrt(grade ** slope) + 1 for grade in range(1, count + 1)]
    largest = most if full else min(most, max(-(-total // count), total * weights[0] // sum(weights)))
    least = 1 if total - largest >= count - 1 else 0
    given, rest = [largest] + [least] * (count - 1), total - largest - least * (count - 1)
    while rest > 0:
        candidates = [i for i in range(1, count) if given[i] < largest] or [i for i in range(1, count) if given[i] < most]
        pool, left = sum([weights[i] for i in candidates]), rest
        for i in candidates:
            extra = min(most - given[i], max(1, left * weights[i] // pool), rest)
            given[i] = given[i] + extra
            rest = rest - extra
    return np.array(given)


def normal_values(key, extent, spread, bound, pieces=(), kind=jnp.bfloat16):
    factor_of = levels(key, extent, pieces, -0.22, 0.18) if pieces else 1.0
    array = jax.random.normal(key, extent, jnp.float32) * spread * factor_of
    return jnp.minimum(jnp.maximum(array, -bound), bound).astype(kind)


def setup_inputs(seed: int = 0) -> dict:
    splits = jax.random.split(jax.random.key(seed), 9)
    vis_values = normal_values(splits[0], (2, VIS), 1.0, 6.0, ((1, 32),), jnp.float32)
    time_block = plant(jax.random.randint(splits[1], (VIS,), 0, TBLK), jax.random.fold_in(splits[1], 1), 0, TBLK - 1).astype(jnp.int32)
    block_gains = normal_values(splits[2], (2, TBLK), 1.0, 4.0, (), jnp.float32)
    target_tile_keys = jax.random.split(jax.random.fold_in(splits[3], 1), VIS // VIS_DEV)
    target_tile_turns = jax.random.permutation(jax.random.fold_in(splits[3], 3), VIS // VIS_DEV)
    target_tile = jax.vmap(lambda own, number: assign_block(jax.random.fold_in(splits[3], 2), own, number, VIS_DEV, TILES, 1, CAP, 2))(target_tile_keys, target_tile_turns).reshape((VIS, 1))
    cell_row = plant(jax.random.randint(splits[4], (VIS,), 0, ROWS_BAND), jax.random.fold_in(splits[4], 1), 0, ROWS_BAND - 1).astype(jnp.int32)
    cell_column = plant(jax.random.randint(splits[5], (VIS,), 0, COLS_BLOCK), jax.random.fold_in(splits[5], 1), 0, COLS_BLOCK - 1).astype(jnp.int32)
    offsets = plant(jax.random.randint(splits[6], (2, VIS), 0, OVER), jax.random.fold_in(splits[6], 1), 0, OVER - 1).astype(jnp.int32)
    kernel = jnp.clip(jax.random.uniform(splits[7], (OVER, KSUP), jnp.float32, 0.1, 1.0), 0.1, 1.0)
    return dict(vis_values=vis_values, time_block=time_block, block_gains=block_gains, target_tile=target_tile, cell_row=cell_row, cell_column=cell_column, offsets=offsets, kernel=kernel)


def reference(vis_values, time_block, block_gains, target_tile, cell_row, cell_column, offsets, kernel):
    gain_real = block_gains[0][time_block]
    gain_imag = block_gains[1][time_block]
    corrected_real = gain_real * vis_values[0] - gain_imag * vis_values[1]
    corrected_imag = gain_real * vis_values[1] + gain_imag * vis_values[0]
    target = target_tile[:, 0]
    first_row = target % N_BAND * ROWS_BAND + cell_row
    first_column = target // N_BAND * COLS_BLOCK + cell_column
    row_table = kernel[offsets[0]]
    column_table = kernel[offsets[1]]
    weights_real = lax.optimization_barrier((corrected_real[:, None] * row_table).astype(jnp.bfloat16)).astype(jnp.float32)
    weights_imag = lax.optimization_barrier((corrected_imag[:, None] * row_table).astype(jnp.bfloat16)).astype(jnp.float32)
    column_weights = lax.optimization_barrier(column_table.astype(jnp.bfloat16)).astype(jnp.float32)
    reach = jnp.arange(KSUP, dtype=jnp.int32)
    row_cells = ((first_row[:, None] + reach[None, :]) % GRID).astype(jnp.int32)
    column_cells = ((first_column[:, None] + reach[None, :]) % GRID).astype(jnp.int32)
    block_size = math.gcd(VIS, 65536)
    block_total = VIS // block_size

    def add_block(uv_grid, portion):
        part_real, part_imag, part_columns, part_rowcells, part_colcells = portion
        flat_rows = jnp.broadcast_to(part_rowcells[:, :, None], (block_size, KSUP, KSUP)).reshape(-1)
        flat_columns = jnp.broadcast_to(part_colcells[:, None, :], (block_size, KSUP, KSUP)).reshape(-1)
        value_real = (part_real[:, :, None] * part_columns[:, None, :]).reshape(-1)
        value_imag = (part_imag[:, :, None] * part_columns[:, None, :]).reshape(-1)
        uv_grid = uv_grid.at[0, flat_rows, flat_columns].add(value_real)
        uv_grid = uv_grid.at[1, flat_rows, flat_columns].add(value_imag)
        return (uv_grid, None)
    portions = (weights_real.reshape(block_total, block_size, KSUP), weights_imag.reshape(block_total, block_size, KSUP), column_weights.reshape(block_total, block_size, KSUP), row_cells.reshape(block_total, block_size, KSUP), column_cells.reshape(block_total, block_size, KSUP))
    uv_grid, _ = lax.scan(add_block, jnp.zeros((2, GRID, GRID), jnp.float32), portions)
    uv_field = uv_grid[0] + 1j * uv_grid[1]
    transformed = jnp.fft.ifft2(uv_field) * (GRID * GRID / (6.0 * math.sqrt(VIS)))
    return jnp.stack([jnp.real(transformed), jnp.imag(transformed)]).astype(jnp.float32)
```

```python
import math

import jax
import jax.numpy as jnp
from jax import lax
from jax.experimental import pallas as pl
from jax.experimental.pallas import tpu as pltpu
from jax.sharding import PartitionSpec as P

GRID = 8192
CHUNK = 256
WINDOW = 256
ALIGN = 128
ROW_STEP = 64
GATHERED = 131072
FIRST = 128


def phase_pair(products, modulus):
    phase_angle = 2.0 * math.pi / modulus * (products % modulus).astype(jnp.float32)
    return (jnp.cos(phase_angle), jnp.sin(phase_angle))


def spread_cyclic(table, shift):
    for bit in (1, 2, 4):
        table = jnp.where((shift & bit) != 0, pltpu.roll(table, bit, 0), table)
    return table


def grid_kernel(low_ref, count_ref, data_ref, taps_ref, fine_ref, coarse_ref, acc_ref, left_ref):
    total = data_ref.shape[1]
    rows = fine_ref.shape[0] // 2
    distinct = coarse_ref.shape[0] // 2
    support = taps_ref.shape[0] // 4
    levels = taps_ref.shape[1]
    reach_rows = fine_ref.shape[1] // 2

    def clear(step, carry):
        acc_ref[pl.ds(pl.multiple_of(step * ALIGN, ALIGN), ALIGN), :] = jnp.zeros(
            (ALIGN, acc_ref.shape[1]), jnp.float32
        )
        return carry

    lax.fori_loop(0, acc_ref.shape[0] // ALIGN, clear, 0)

    def chunk(step, carry):
        data = data_ref[:, pl.ds(pl.multiple_of(step * CHUNK, CHUNK), CHUNK)]
        whole = data[2:6].astype(jnp.int32)
        row, column, row_offset, column_offset = (whole[k : k + 1] for k in range(4))
        level = lax.broadcasted_iota(jnp.int32, (levels, CHUNK), 0)
        row_hot = jnp.where(level == row_offset, 1.0, 0.0).astype(jnp.bfloat16)
        column_hot = jnp.where(level == column_offset, 1.0, 0.0).astype(jnp.bfloat16)
        row_taps = jnp.dot(taps_ref[...], row_hot, preferred_element_type=jnp.float32)
        column_taps = jnp.dot(taps_ref[...], column_hot, preferred_element_type=jnp.float32)
        row_taps = (row_taps[:support] + row_taps[support : 2 * support]) + row_taps[
            2 * support : 3 * support
        ]
        row_taps = spread_cyclic(row_taps, row & 7)
        column_taps = spread_cyclic(column_taps[3 * support :], column & 7)
        fine = row & (ROW_STEP - 1)
        reach = lax.broadcasted_iota(jnp.int32, (reach_rows, CHUNK), 0) - fine
        inside = (reach >= 0) & (reach < support)
        placed = []
        for part in range(2):
            weights = (data[part : part + 1] * row_taps).astype(jnp.bfloat16).astype(jnp.float32)
            tiled = jnp.concatenate([weights] * (reach_rows // support), axis=0)
            placed.append(jnp.where(inside, tiled, 0.0))
        placed = jnp.concatenate(placed, axis=0).astype(jnp.bfloat16)
        turned = jnp.dot(fine_ref[...], placed, preferred_element_type=jnp.float32)
        coarse_level = lax.broadcasted_iota(jnp.int32, (GRID // ROW_STEP, CHUNK), 0)
        coarse_hot = jnp.where(coarse_level == row // ROW_STEP, 1.0, 0.0).astype(jnp.bfloat16)
        coarse_hot = jnp.concatenate([coarse_hot, coarse_hot], axis=0)
        phase = jnp.dot(coarse_ref[...], coarse_hot, preferred_element_type=jnp.float32)
        phase_cos, phase_sin = phase[:distinct], phase[distinct:]
        for part in range(rows // distinct):
            real = turned[part * distinct : (part + 1) * distinct]
            imag = turned[rows + part * distinct : rows + (part + 1) * distinct]
            left_ref[part * distinct : (part + 1) * distinct, :] = (
                real * phase_cos - imag * phase_sin
            ).astype(jnp.bfloat16)
            left_ref[rows + part * distinct : rows + (part + 1) * distinct, :] = (
                real * phase_sin + imag * phase_cos
            ).astype(jnp.bfloat16)
        low = low_ref[step]

        def window(number, inner):
            base = pl.multiple_of(low + number * WINDOW, ALIGN)
            ahead = lax.broadcasted_iota(jnp.int32, (WINDOW, CHUNK), 0) - (column - base)
            tiled = jnp.concatenate([column_taps] * (WINDOW // support), axis=0)
            right = jnp.where((ahead >= 0) & (ahead < support), tiled, 0.0).astype(jnp.bfloat16)
            acc_ref[pl.ds(base, WINDOW), :] += lax.dot_general(
                right,
                left_ref[...],
                (((1,), (1,)), ((), ())),
                preferred_element_type=jnp.float32,
            )
            return inner

        lax.fori_loop(0, count_ref[step], window, 0)
        return carry

    lax.fori_loop(0, total // CHUNK, chunk, 0)
    acc_ref[:support, :] += acc_ref[GRID : GRID + support, :]


def grid_rows(data, taps, fine_table, coarse_table):
    columns = data[3].astype(jnp.int32).reshape(-1, CHUNK)
    low = jnp.min(columns, axis=1) // ALIGN * ALIGN
    support = taps.shape[0] // 4
    count = (jnp.max(columns, axis=1) + support - 1 - low) // WINDOW + 1
    width = fine_table.shape[0]
    in_smem = pl.BlockSpec(memory_space=pltpu.SMEM)
    in_vmem = pl.BlockSpec(memory_space=pltpu.VMEM)
    return pl.pallas_call(
        grid_kernel,
        out_shape=jax.ShapeDtypeStruct((GRID + WINDOW, width), jnp.float32),
        in_specs=[in_smem] * 2 + [in_vmem] * 4,
        out_specs=in_vmem,
        scratch_shapes=[pltpu.VMEM((width, CHUNK), jnp.bfloat16)],
        compiler_params=pltpu.CompilerParams(vmem_limit_bytes=48 * 1024 * 1024),
        name="grid_rows",
    )(low, count, data, taps, fine_table, coarse_table)


def transform_columns(columns, rows, scale):
    second = GRID // FIRST
    first_index = jnp.arange(FIRST, dtype=jnp.int32)
    second_index = jnp.arange(second, dtype=jnp.int32)
    arranged = columns.reshape(FIRST, second, 2 * rows)
    table = jnp.concatenate(
        phase_pair(first_index[:, None] * first_index[None, :], FIRST), axis=1
    )
    mixed = jnp.einsum("vk,vwx->kwx", table, arranged, precision=lax.Precision.HIGH)
    real = mixed[:FIRST, :, :rows] - mixed[FIRST:, :, rows:]
    imag = mixed[FIRST:, :, :rows] + mixed[:FIRST, :, rows:]
    twist_cos, twist_sin = phase_pair(first_index[:, None] * second_index[None, :], GRID)
    twist_cos, twist_sin = twist_cos[:, :, None], twist_sin[:, :, None]
    turned = jnp.concatenate(
        [real * twist_cos - imag * twist_sin, real * twist_sin + imag * twist_cos], axis=2
    )
    table = jnp.concatenate(
        phase_pair(second_index[:, None] * second_index[None, :], second), axis=1
    )
    mixed = jnp.einsum("wk,qwx->kqx", table, turned, precision=lax.Precision.HIGH)
    real = mixed[:second, :, :rows] - mixed[second:, :, rows:]
    imag = mixed[second:, :, :rows] + mixed[:second, :, rows:]
    image = jnp.stack([real, imag]) * scale
    return jnp.transpose(image, (0, 3, 1, 2)).reshape(2, rows, GRID)


def local(vis_values, time_block, block_gains, target_tile, cell_row, cell_column, offsets, kernel):
    vis_devices = lax.axis_size("vis")
    band_devices = lax.axis_size("band")
    devices = vis_devices * band_devices
    held_count = vis_values.shape[1]
    rows_band = GRID // band_devices
    cols_block = GRID // vis_devices
    rows = GRID // devices
    support = kernel.shape[1]
    oversample = kernel.shape[0]
    pick = time_block[None, :] == jnp.arange(block_gains.shape[1], dtype=jnp.int32)[:, None]
    gain_real = jnp.sum(jnp.where(pick, block_gains[0][:, None], 0.0), axis=0)
    gain_imag = jnp.sum(jnp.where(pick, block_gains[1][:, None], 0.0), axis=0)
    corrected_real = gain_real * vis_values[0] - gain_imag * vis_values[1]
    corrected_imag = gain_real * vis_values[1] + gain_imag * vis_values[0]
    target = target_tile[:, 0]
    first_row = target % band_devices * rows_band + cell_row
    first_column = target // band_devices * cols_block + cell_column
    cell, offset, corrected_real, corrected_imag = lax.sort(
        (
            first_column * GRID + first_row,
            offsets[0] * oversample + offsets[1],
            corrected_real,
            corrected_imag,
        ),
        num_keys=1,
        is_stable=False,
    )
    held = jnp.stack(
        [corrected_real, corrected_imag]
        + [
            index.astype(jnp.float32)
            for index in (cell % GRID, cell // GRID, offset // oversample, offset % oversample)
        ]
    )

    taps = kernel.T
    split, rest = [], taps
    for _ in range(3):
        split.append(lax.reduce_precision(rest, 8, 7))
        rest = rest - split[-1]
    taps = jnp.concatenate(split + [split[0]]).astype(jnp.bfloat16)

    own = (lax.axis_index("vis") * band_devices + lax.axis_index("band")) * rows
    row_index = own + jnp.arange(rows, dtype=jnp.int32)
    reach = jnp.arange(ROW_STEP + support, dtype=jnp.int32)
    fine_cos, fine_sin = phase_pair(row_index[:, None] * reach[None, :], GRID)
    fine_table = jnp.concatenate(
        [
            jnp.concatenate([fine_cos, -fine_sin], axis=1),
            jnp.concatenate([fine_sin, fine_cos], axis=1),
        ]
    ).astype(jnp.bfloat16)
    coarse_count = GRID // ROW_STEP
    distinct = min(rows, coarse_count)
    coarse_table = jnp.concatenate(
        phase_pair(
            row_index[:distinct, None] * jnp.arange(coarse_count, dtype=jnp.int32)[None, :],
            coarse_count,
        )
    )
    coarse_high = lax.reduce_precision(coarse_table, 8, 7)
    coarse_table = jnp.concatenate([coarse_high, coarse_table - coarse_high], axis=1).astype(
        jnp.bfloat16
    )

    pieces = max(1, held_count * devices // GATHERED)
    piece = held_count // pieces

    def grid_piece(part):
        data = lax.all_gather(part, ("vis", "band"), axis=1, tiled=True)
        return grid_rows(data, taps, fine_table, coarse_table)

    if pieces == 1:
        gridded = grid_piece(held)
    else:
        parts = jnp.moveaxis(held.reshape(held.shape[0], pieces, piece), 1, 0)
        gridded, _ = lax.scan(
            lambda running, part: (running + grid_piece(part), None),
            jnp.zeros((GRID + WINDOW, 2 * rows), jnp.float32),
            parts,
        )
    sky_scale = 1.0 / (6.0 * math.sqrt(held_count * devices))
    return transform_columns(gridded[:GRID], rows, sky_scale)


def solution(mesh):
    in_specs = (
        P(None, ("vis", "band")),
        P(("vis", "band")),
        P(),
        P(("vis", "band"), None),
        P(("vis", "band")),
        P(("vis", "band")),
        P(None, ("vis", "band")),
        P(),
    )
    out_specs = P(None, ("vis", "band"), None)
    return jax.shard_map(local, mesh=mesh, in_specs=in_specs, out_specs=out_specs, check_vma=False)
```
